32 devices in a mesh: groups: 2 (over x), factor: 16 (over z, y, core).
Axes of the slice: x: 2, y: 2, z: 4, core: 2. Of those that a mesh axis runs over, the one named last changes fastest.
Arguments:
- history: bfloat16 [640, 32768], P(None, 'factor'), may hold values from -6 to 6
- scenario_ids: int32 [2048], P('groups'), parts along dimension 0, may hold values from 0 to 639
- desk_ids: int32 [4096], P(('groups', 'factor')), parts along dimension 0, may hold values from 0 to 15, as said below
- column_ids: int32 [4096], P(('groups', 'factor')), parts along dimension 0, may hold values from 0 to 15
- live_count: int32 [32], P(('groups', 'factor')), parts along dimension 0, may hold values from 16 to 128, as said below
- delta_blocks: bfloat16 [4096, 128, 128], P(('groups', 'factor')), parts along dimension 0, may hold values from -0.078125 to 0.078125
- gamma_blocks: bfloat16 [4096, 128, 128], P(('groups', 'factor')), parts along dimension 0, may hold values from -0.078125 to 0.078125
Outputs:
- pnl: float32 [4096, 1024], P(('groups', 'factor')), parts along dimension 0
- book_total: float32 [2048], P('groups'), parts along dimension 0
The draws below stay inside these ranges and needn't reach their ends.
There are 2 independent parts, one for each index of `groups`. The reference program is written for one: setup_inputs(seed, part) draws one part's arguments, and reference() takes and returns one part's arrays. A program takes and returns all parts, laid end to end along the dimension named above; an argument that names none is the same for every part. Nothing has to cross between parts.
Inputs may be any that keep to these rules, and one draw needn't show every extreme that they name: `desk_ids`: the desk of a slot held by index p of factor is (p + o) mod 16 for some o from -4 to 4. `live_count`: one index of factor holds exactly 128 live slots; slots at or past the count are ignored.
All inputs are finite; a program needn't handle non-finite values.
Results may differ from the reference program's by a relative error of at most 0.002.
Values sent between devices are 32-bit elements; how exact they have to be, the bound alone decides.
A program may use at most 64 MiB of HBM per device.

```python
import jax
import jax.numpy as jnp
from jax import lax

BLOCK = 128
DESK_ROWS = 128
REACH = 4
FBD = 16
S = 1024
DAYS = 640
NNZ_DEV = 128
FACTORS = 32768
SLOTS = 2048
N_FACTOR = 16


def draw_desk_ids(key, part):
    key = jax.random.fold_in(key, 5)
    offsets = jax.random.randint(key, (N_FACTOR, NNZ_DEV), -REACH, REACH + 1)
    owners = jnp.arange(N_FACTOR, dtype=jnp.int32)[:, None]
    desks = (owners + offsets + N_FACTOR) % N_FACTOR
    return desks.reshape(N_FACTOR * NNZ_DEV).astype(jnp.int32)


def draw_column_ids(key, part):
    key = jax.random.fold_in(key, 7)
    return jax.random.randint(key, (N_FACTOR * NNZ_DEV,), 0, FBD).astype(jnp.int32)


def draw_live_count(key, part):
    key = jax.random.fold_in(key, 11)
    first_key, second_key = jax.random.split(key)
    raw_draw = jax.random.randint(first_key, (N_FACTOR,), 0, NNZ_DEV + 1)
    counts = jnp.maximum(max(1, NNZ_DEV // 8), raw_draw * raw_draw // NNZ_DEV)
    busiest = jax.random.randint(second_key, (), 0, N_FACTOR)
    positions = jnp.arange(N_FACTOR, dtype=jnp.int32)
    return jnp.where(positions == busiest, NNZ_DEV, counts).astype(jnp.int32)


def set_ends(array, own_key, least, high):
    place = [jax.random.randint(jax.random.fold_in(own_key, axis), (), 0, length) for axis, length in enumerate(array.shape)]
    longest = array.shape.index(max(array.shape))
    neighbour = place[:longest] + [(place[longest] + 1) % array.shape[longest]] + place[longest + 1:]
    return array.at[tuple(place)].set(least).at[tuple(neighbour)].set(high)


def block_levels(stream_key, shape, shards, least, high):
    def one(position, blocks):
        draws = jax.random.uniform(jax.random.fold_in(jax.random.fold_in(stream_key, 6), position), (blocks,), jnp.float32, least / len(shards), high / len(shards))
        return jnp.repeat(jnp.exp(draws), shape[position] // blocks).reshape((-1,) + (1,) * (len(shape) - position - 1))

    gain = one(*shards[0])
    for cut in shards[1:]:
        gain = gain * one(*cut)
    return gain


def gaussian(key, shape, scale, bound, cuts=(), kind=jnp.bfloat16):
    level = block_levels(key, shape, cuts, -0.22, 0.18) if cuts else 1.0
    array = jax.random.normal(key, shape, jnp.float32) * scale * level
    return jnp.minimum(jnp.maximum(array, -bound), bound).astype(kind)


def setup_inputs(seed: int = 0, part: int = 0) -> dict:
    key_list = jax.random.split(jax.random.key(seed), 8)
    part_splits = jax.random.split(jax.random.fold_in(key_list[7], part), 8)
    return {
        "history": gaussian(key_list[0], (DAYS, FACTORS), 1.0, 6.0, ((1, 16),)),
        "scenario_ids": set_ends(jax.random.randint(part_splits[1], (S,), 0, DAYS), jax.random.fold_in(part_splits[1], 1), 0, DAYS - 1).astype(jnp.int32),
        "desk_ids": draw_desk_ids(jax.random.fold_in(jax.random.fold_in(key_list[7], part), 71), part),
        "column_ids": draw_column_ids(jax.random.fold_in(jax.random.fold_in(key_list[7], part), 71), part),
        "live_count": draw_live_count(jax.random.fold_in(jax.random.fold_in(key_list[7], part), 71), part),
        "delta_blocks": gaussian(part_splits[5], (SLOTS, DESK_ROWS, BLOCK), (NNZ_DEV * BLOCK // 3) ** -0.5, 0.078125, ((0, 16),)),
        "gamma_blocks": gaussian(part_splits[6], (SLOTS, DESK_ROWS, BLOCK), (NNZ_DEV * BLOCK // 3) ** -0.5, 0.078125, ((0, 16),)),
    }


def reference(history, scenario_ids, desk_ids, column_ids, live_count, delta_blocks, gamma_blocks):
    shocks = jnp.take(history, scenario_ids, axis=0)
    half_square = (0.5 * jnp.square(shocks.astype(jnp.float32))).astype(jnp.bfloat16)
    scenarios = scenario_ids.shape[0]
    shock_tiles = shocks.reshape(scenarios, N_FACTOR * FBD, BLOCK)
    square_tiles = half_square.reshape(scenarios, N_FACTOR * FBD, BLOCK)
    dims = (((1,), (1,)), ((), ()))

    def step(total, slot):
        owner = slot // NNZ_DEV
        within = slot - owner * NNZ_DEV
        alive = within < live_count[owner]
        block = (owner * FBD + column_ids[slot]).astype(jnp.int32)
        shock_part = lax.dynamic_index_in_dim(shock_tiles, block, 1, keepdims=False)
        square_part = lax.dynamic_index_in_dim(square_tiles, block, 1, keepdims=False)
        delta_part = lax.dynamic_index_in_dim(delta_blocks, slot, 0, keepdims=False)
        gamma_part = lax.dynamic_index_in_dim(gamma_blocks, slot, 0, keepdims=False)
        term = lax.dot_general(delta_part, shock_part, dims, preferred_element_type=jnp.float32)
        term = term + lax.dot_general(gamma_part, square_part, dims, preferred_element_type=jnp.float32)
        term = jnp.where(alive, term, jnp.zeros_like(term))
        offset = (desk_ids[slot] * DESK_ROWS).astype(jnp.int32)
        current = lax.dynamic_slice_in_dim(total, offset, DESK_ROWS, 0)
        return (lax.dynamic_update_slice_in_dim(total, current + term, offset, 0), None)
    start_total = jnp.zeros((N_FACTOR * DESK_ROWS, scenarios), jnp.float32)
    pnl, _ = lax.scan(step, start_total, jnp.arange(N_FACTOR * NNZ_DEV, dtype=jnp.int32))
    book_total = lax.optimization_barrier(jnp.sum(pnl, axis=0)) / jnp.sqrt(jnp.float32(N_FACTOR * DESK_ROWS))
    return (pnl, book_total)
```

```python
import functools
import math

import jax
import jax.numpy as jnp
from jax import lax
from jax.experimental import pallas as pl
from jax.experimental.pallas import tpu as pltpu
from jax.sharding import PartitionSpec as P

REACH = 4
SPAN = 2 * REACH + 1
CHUNK = 8
MIB = 1 << 20


def block_kernel(devices, desks, columns, live, hist_ref, delta_ref, gamma_ref, tiles_ref, days):
    step = pl.program_id(0)
    position = lax.axis_index("factor")
    chunk, _, width = delta_ref.shape

    @pl.when(step == 0)
    def _():
        tiles_ref[...] = jnp.zeros_like(tiles_ref)
        for c in range(days.shape[0]):
            shock = hist_ref[:, c * width:(c + 1) * width]
            wide = shock.astype(jnp.float32)
            days[c, :, :width] = shock
            days[c, :, width:] = (0.5 * (wide * wide)).astype(jnp.bfloat16)

    for i in range(chunk):
        slot = step * chunk + i

        @pl.when(slot < live[0])
        def _():
            tile = lax.rem(desks[slot] - position + (REACH + devices), devices)
            block = jnp.concatenate([delta_ref[i], gamma_ref[i]], axis=1)
            tiles_ref[tile] += lax.dot_general(
                days[columns[slot]], block, (((1,), (1,)), ((), ())),
                preferred_element_type=jnp.float32,
            )


def split(value):
    high = value.astype(jnp.bfloat16)
    return high, (value - high.astype(jnp.float32)).astype(jnp.bfloat16)


def exchange_kernel(n, scale, ids_ref, tiles, pnl_ref, book_ref, even, paired, landed, rows, pick,
                    load_sem, send1, recv1, send2, recv2, send3, recv3):
    me = lax.axis_index("factor")
    core = lax.rem(me, 2)
    sibling = me + 1 - 2 * core

    def at(distance):
        return {"factor": lax.rem(me + distance + n, n)}

    loads = [pltpu.make_async_copy(tiles.at[2 * e], even.at[e], load_sem.at[e]) for e in range(5)]
    for load in loads:
        load.start()

    barrier = pltpu.get_barrier_semaphore()
    for k in range(1, n):
        pl.semaphore_signal(barrier, inc=1, device_id=at(k), device_id_type=pl.DeviceIdType.MESH)
    pl.semaphore_wait(barrier, n - 1)

    pair = [
        pltpu.make_async_remote_copy(
            src_ref=tiles.at[2 * i + 1], dst_ref=paired.at[i],
            send_sem=send1.at[i], recv_sem=recv1.at[i],
            device_id={"factor": sibling}, device_id_type=pl.DeviceIdType.MESH,
        )
        for i in range(4)
    ]
    for i in (3, 0, 1, 2):
        pair[i].start()
    for load in loads:
        load.wait()

    def add_pair(e):
        i = e - 1 + core
        pltpu.make_async_remote_copy(
            src_ref=tiles.at[1], dst_ref=paired.at[i],
            send_sem=send1.at[i], recv_sem=recv1.at[i],
            device_id={"factor": sibling}, device_id_type=pl.DeviceIdType.MESH,
        ).wait_recv()
        even[e] += paired[i]

    out = []
    for s, e in enumerate((0, 4, 1, 3)):
        if e == 0:
            pl.when(core == 1)(functools.partial(add_pair, e))
        elif e == 4:
            pl.when(core == 0)(functools.partial(add_pair, e))
        else:
            add_pair(e)
        copy = pltpu.make_async_remote_copy(
            src_ref=even.at[e], dst_ref=landed.at[s],
            send_sem=send2.at[s], recv_sem=recv2.at[s],
            device_id=at(2 * e - 4), device_id_type=pl.DeviceIdType.MESH,
        )
        copy.start()
        out.append(copy)
    add_pair(2)

    whole = (even[0] + even[1]) + (even[2] + even[3]) + even[4]
    rows[0] = jnp.sum(whole.T, axis=0, keepdims=True)
    share = []
    for k in range(1, n):
        copy = pltpu.make_async_remote_copy(
            src_ref=rows.at[0], dst_ref=rows.at[k],
            send_sem=send3.at[k], recv_sem=recv3.at[k],
            device_id=at(k), device_id_type=pl.DeviceIdType.MESH,
        )
        copy.start()
        share.append(copy)
    day = lax.broadcasted_iota(jnp.int32, pick.shape, 0)
    pick[...] = (day == ids_ref[...]).astype(jnp.float32).astype(jnp.bfloat16)
    for copy in share:
        copy.wait()
    total = rows[0]
    for k in range(1, n):
        total += rows[k]
    high, rest = split(jnp.broadcast_to(total, (16, total.shape[1])))
    book = jnp.dot(high, pick[...], preferred_element_type=jnp.float32)
    book += jnp.dot(rest, pick[...], preferred_element_type=jnp.float32)
    book_ref[...] = book[0:1] * scale

    final = even[2]
    for s, copy in enumerate(out):
        copy.wait()
        final += landed[s]
    high, rest = split(final.T)
    pnl_ref[...] = jnp.dot(high, pick[...], preferred_element_type=jnp.float32) + jnp.dot(
        rest, pick[...], preferred_element_type=jnp.float32
    )
    for copy in pair:
        copy.wait_send()


def per_device(devices, history, scenario_ids, desk_ids, column_ids, live_count, delta_blocks, gamma_blocks):
    day_count, factors = history.shape
    slots, desk_rows, width = delta_blocks.shape
    columns = factors // width
    scenarios = scenario_ids.shape[0]

    tiles = pl.pallas_call(
        functools.partial(block_kernel, devices),
        grid_spec=pltpu.PrefetchScalarGridSpec(
            num_scalar_prefetch=3,
            grid=(slots // CHUNK,),
            in_specs=[
                pl.BlockSpec((day_count, factors), lambda g, *_: (0, 0)),
                pl.BlockSpec((CHUNK, desk_rows, width), lambda g, *_: (g, 0, 0)),
                pl.BlockSpec((CHUNK, desk_rows, width), lambda g, *_: (g, 0, 0)),
            ],
            out_specs=pl.BlockSpec((SPAN, day_count, desk_rows), lambda g, *_: (0, 0, 0)),
            scratch_shapes=[pltpu.VMEM((columns, day_count, 2 * width), jnp.bfloat16)],
        ),
        out_shape=jax.ShapeDtypeStruct((SPAN, day_count, desk_rows), jnp.float32),
        compiler_params=pltpu.CompilerParams(vmem_limit_bytes=40 * MIB),
        name="block_products",
    )(desk_ids, column_ids, live_count, history, delta_blocks, gamma_blocks)

    f32 = jnp.float32
    tile = (day_count, desk_rows)
    pnl, book = pl.pallas_call(
        functools.partial(exchange_kernel, devices, 1.0 / math.sqrt(devices * desk_rows)),
        in_specs=[pl.BlockSpec(memory_space=pltpu.VMEM), pl.BlockSpec(memory_space=pl.ANY)],
        out_specs=[pl.BlockSpec(memory_space=pltpu.VMEM)] * 2,
        out_shape=[
            jax.ShapeDtypeStruct((desk_rows, scenarios), f32),
            jax.ShapeDtypeStruct((1, scenarios), f32),
        ],
        scratch_shapes=[
            pltpu.VMEM((5, *tile), f32),
            pltpu.VMEM((4, *tile), f32),
            pltpu.VMEM((4, *tile), f32),
            pltpu.VMEM((devices, 1, day_count), f32),
            pltpu.VMEM((day_count, scenarios), jnp.bfloat16),
            pltpu.SemaphoreType.DMA((5,)),
            pltpu.SemaphoreType.DMA((4,)),
            pltpu.SemaphoreType.DMA((4,)),
            pltpu.SemaphoreType.DMA((4,)),
            pltpu.SemaphoreType.DMA((4,)),
            pltpu.SemaphoreType.DMA((devices,)),
            pltpu.SemaphoreType.DMA((devices,)),
        ],
        compiler_params=pltpu.CompilerParams(
            collective_id=0, has_side_effects=True, vmem_limit_bytes=40 * MIB
        ),
        name="desk_exchange",
    )(scenario_ids.reshape(1, scenarios), tiles)
    return pnl, book.reshape(scenarios)


def solution(mesh):
    return jax.shard_map(
        functools.partial(per_device, mesh.shape["factor"]),
        mesh=mesh,
        in_specs=(
            P(None, "factor"),
            P("groups"),
            P(("groups", "factor")),
            P(("groups", "factor")),
            P(("groups", "factor")),
            P(("groups", "factor"), None, None),
            P(("groups", "factor"), None, None),
        ),
        out_specs=(P(("groups", "factor"), None), P("groups")),
        check_vma=False,
    )
```

```python
import functools
import math

import jax
import jax.numpy as jnp
from jax import lax
from jax.experimental import pallas as pl
from jax.experimental.pallas import tpu as pltpu
from jax.sharding import PartitionSpec as P

REACH = 4
SPAN = 2 * REACH + 1
CHUNK = 16
BATCH = 8
MIB = 1 << 20


def block_kernel(devices, desks, columns, live, hist_ref, delta_ref, gamma_ref, tiles_ref, days):
    step = pl.program_id(0)
    position = lax.axis_index("factor")
    chunk, _, width = delta_ref.shape

    @pl.when(step == 0)
    def _():
        tiles_ref[...] = jnp.zeros_like(tiles_ref)
        for c in range(days.shape[0]):
            shock = hist_ref[:, c * width:(c + 1) * width]
            wide = shock.astype(jnp.float32)
            days[c, :, :width] = shock
            days[c, :, width:] = (0.5 * (wide * wide)).astype(jnp.bfloat16)

    for base in range(0, chunk, BATCH):

        @pl.when(step * chunk + base < live[0])
        def _():
            for i in range(base, base + BATCH):
                slot = step * chunk + i
                tile = lax.rem(desks[slot] - position + (REACH + devices), devices)
                block = jnp.concatenate([delta_ref[i], gamma_ref[i]], axis=1)
                block = jnp.where(slot < live[0], block, jnp.zeros_like(block))
                tiles_ref[tile] += lax.dot_general(
                    days[columns[slot]], block, (((1,), (1,)), ((), ())),
                    preferred_element_type=jnp.float32,
                )


def split(value):
    high = value.astype(jnp.bfloat16)
    return high, (value - high.astype(jnp.float32)).astype(jnp.bfloat16)


def exchange_kernel(n, scale, ids_ref, tiles, pnl_ref, book_ref, even, paired, middle, landed, rows, pick,
                    load_sem, send1, recv1, send2, recv2, send3, recv3, send4, recv4):
    me = lax.axis_index("factor")
    core = lax.rem(me, 2)
    side = lax.rem(me // 2, 2)
    sibling = me + 1 - 2 * core
    partner = me + 2 - 4 * side
    half = even.shape[1] // 2
    parts = [pl.ds(h * half, half) for h in range(2)]

    def at(distance):
        return {"factor": lax.rem(me + distance + n, n)}

    def remote(src, dst, send, recv, device):
        return pltpu.make_async_remote_copy(
            src_ref=src, dst_ref=dst, send_sem=send, recv_sem=recv,
            device_id=device, device_id_type=pl.DeviceIdType.MESH,
        )

    def place(k):
        return k + side * (4 - 2 * k)

    loads = [pltpu.make_async_copy(tiles.at[2 * e], even.at[e], load_sem.at[e]) for e in range(5)]
    for load in loads:
        load.start()

    barrier = pltpu.get_barrier_semaphore()
    for k in range(1, n):
        pl.semaphore_signal(barrier, inc=1, device_id=at(k), device_id_type=pl.DeviceIdType.MESH)
    pl.semaphore_wait(barrier, n - 1)

    def pair(i):
        return remote(tiles.at[2 * i + 1], paired.at[i], send1.at[i], recv1.at[i], {"factor": sibling})

    def if_paired(k, owner, act):
        if k == 0:
            pl.when(owner == 1 - side)(act)
        elif k == 4:
            pl.when(owner == side)(act)
        else:
            act()

    order = (0, 1, 3, 4, 2)
    for k in order:
        if_paired(k, 1 - core, lambda: pair(place(k) - core).start())
    for load in loads:
        load.wait()

    def add_pair(k):
        e = place(k)

        def act():
            i = e - 1 + core
            pair(i).wait_recv()
            even[e] += paired[i]

        if_paired(k, core, act)

    def straight(k, slot, part):
        e = place(k)
        return remote(even.at[e, part], landed.at[slot, part], send2.at[slot, part.start // half],
                      recv2.at[slot, part.start // half], at(2 * e - 4))

    def across(k, slot, part):
        return remote(even.at[place(k), part], middle.at[slot, part], send3.at[slot, part.start // half],
                      recv3.at[slot, part.start // half], {"factor": partner})

    add_pair(0)
    first = [straight(0, 0, part) for part in parts]
    for copy in first:
        copy.start()
    add_pair(1)
    joined = [across(1, 0, part) for part in parts]
    for copy in joined:
        copy.start()
    add_pair(3)
    owned = [across(3, 1, part) for part in parts]
    for copy in owned:
        copy.start()
    add_pair(4)
    add_pair(2)

    whole = (even[0] + even[1]) + (even[2] + even[3]) + even[4]
    rows[0] = jnp.sum(whole.T, axis=0, keepdims=True)
    share = [remote(rows.at[0], rows.at[k], send4.at[k], recv4.at[k], at(k)) for k in range(1, n)]

    second = [straight(4, 1, part) for part in parts]
    for h, part in enumerate(parts):
        joined[h].wait_recv()
        even[place(4), part] += middle[0, part]
        second[h].start()
    for copy in share:
        copy.start()

    day = lax.broadcasted_iota(jnp.int32, pick.shape, 0)
    pick[...] = (day == ids_ref[...]).astype(jnp.float32).astype(jnp.bfloat16)
    for copy in share:
        copy.wait()
    total = rows[0]
    for k in range(1, n):
        total += rows[k]
    high, rest = split(jnp.broadcast_to(total, (16, total.shape[1])))
    book = jnp.dot(high, pick[...], preferred_element_type=jnp.float32)
    book += jnp.dot(rest, pick[...], preferred_element_type=jnp.float32)
    book_ref[...] = book[0:1] * scale

    for copy in owned + first:
        copy.wait()
    even[2] += middle[1] + landed[0]
    for copy in second:
        copy.wait()
    high, rest = split((even[2] + landed[1]).T)
    pnl_ref[...] = jnp.dot(high, pick[...], preferred_element_type=jnp.float32) + jnp.dot(
        rest, pick[...], preferred_element_type=jnp.float32
    )
    for copy in joined:
        copy.wait_send()
    for k in order:
        if_paired(k, 1 - core, lambda: pair(place(k) - core).wait_send())


def per_device(devices, history, scenario_ids, desk_ids, column_ids, live_count, delta_blocks, gamma_blocks):
    day_count, factors = history.shape
    slots, desk_rows, width = delta_blocks.shape
    columns = factors // width
    scenarios = scenario_ids.shape[0]

    tiles = pl.pallas_call(
        functools.partial(block_kernel, devices),
        grid_spec=pltpu.PrefetchScalarGridSpec(
            num_scalar_prefetch=3,
            grid=(slots // CHUNK,),
            in_specs=[
                pl.BlockSpec((day_count, factors), lambda g, *_: (0, 0)),
                pl.BlockSpec((CHUNK, desk_rows, width), lambda g, *_: (g, 0, 0)),
                pl.BlockSpec((CHUNK, desk_rows, width), lambda g, *_: (g, 0, 0)),
            ],
            out_specs=pl.BlockSpec((SPAN, day_count, desk_rows), lambda g, *_: (0, 0, 0)),
            scratch_shapes=[pltpu.VMEM((columns, day_count, 2 * width), jnp.bfloat16)],
        ),
        out_shape=jax.ShapeDtypeStruct((SPAN, day_count, desk_rows), jnp.float32),
        compiler_params=pltpu.CompilerParams(vmem_limit_bytes=60 * MIB),
        name="block_products",
    )(desk_ids, column_ids, live_count, history, delta_blocks, gamma_blocks)

    f32 = jnp.float32
    tile = (day_count, desk_rows)
    pnl, book = pl.pallas_call(
        functools.partial(exchange_kernel, devices, 1.0 / math.sqrt(devices * desk_rows)),
        in_specs=[pl.BlockSpec(memory_space=pltpu.VMEM), pl.BlockSpec(memory_space=pl.ANY)],
        out_specs=[pl.BlockSpec(memory_space=pltpu.VMEM)] * 2,
        out_shape=[
            jax.ShapeDtypeStruct((desk_rows, scenarios), f32),
            jax.ShapeDtypeStruct((1, scenarios), f32),
        ],
        scratch_shapes=[
            pltpu.VMEM((5, *tile), f32),
            pltpu.VMEM((4, *tile), f32),
            pltpu.VMEM((2, *tile), f32),
            pltpu.VMEM((2, *tile), f32),
            pltpu.VMEM((devices, 1, day_count), f32),
            pltpu.VMEM((day_count, scenarios), jnp.bfloat16),
            pltpu.SemaphoreType.DMA((5,)),
            pltpu.SemaphoreType.DMA((4,)),
            pltpu.SemaphoreType.DMA((4,)),
            pltpu.SemaphoreType.DMA((2, 2)),
            pltpu.SemaphoreType.DMA((2, 2)),
            pltpu.SemaphoreType.DMA((2, 2)),
            pltpu.SemaphoreType.DMA((2, 2)),
            pltpu.SemaphoreType.DMA((devices,)),
            pltpu.SemaphoreType.DMA((devices,)),
        ],
        compiler_params=pltpu.CompilerParams(
            collective_id=0, has_side_effects=True, vmem_limit_bytes=40 * MIB
        ),
        name="desk_exchange",
    )(scenario_ids.reshape(1, scenarios), tiles)
    return pnl, book.reshape(scenarios)


def solution(mesh):
    return jax.shard_map(
        functools.partial(per_device, mesh.shape["factor"]),
        mesh=mesh,
        in_specs=(
            P(None, "factor"),
            P("groups"),
            P(("groups", "factor")),
            P(("groups", "factor")),
            P(("groups", "factor")),
            P(("groups", "factor"), None, None),
            P(("groups", "factor"), None, None),
        ),
        out_specs=(P(("groups", "factor"), None), P("groups")),
        check_vma=False,
    )
```

```python
import functools
import math

import jax
import jax.numpy as jnp
from jax import lax
from jax.experimental import pallas as pl
from jax.experimental.pallas import tpu as pltpu
from jax.sharding import PartitionSpec as P

REACH = 4
SPAN = 2 * REACH + 1
CHUNK = 16
HIST_PARTS = 4
PIECES = 4
MIB = 1 << 20


def block_kernel(devices, desks, columns, live, hist_hbm, delta_hbm, gamma_hbm, out_hbm,
                 tiles, days, hist, delta, gamma, hist_sem, block_sem, out_sem):
    position = lax.axis_index("factor")
    slots, _, width = delta.shape
    span = hist.shape[1] // hist_sem.shape[0]

    def hist_copy(h):
        at = pl.ds(h * span, span)
        return pltpu.make_async_copy(hist_hbm.at[:, at], hist.at[:, at], hist_sem.at[h])

    def block_copies(g):
        at = pl.ds(g * CHUNK, CHUNK)
        return [
            pltpu.make_async_copy(delta_hbm.at[at], delta.at[at], block_sem.at[0, g]),
            pltpu.make_async_copy(gamma_hbm.at[at], gamma.at[at], block_sem.at[1, g]),
        ]

    for h in range(hist_sem.shape[0]):
        hist_copy(h).start()
    for g in range(slots // CHUNK):

        @pl.when(g * CHUNK < live[0])
        def _():
            for copy in block_copies(g):
                copy.start()

    tiles[...] = jnp.zeros_like(tiles)
    for h in range(hist_sem.shape[0]):
        hist_copy(h).wait()
        for c in range(h * span // width, (h + 1) * span // width):
            shock = hist[:, c * width:(c + 1) * width]
            wide = shock.astype(jnp.float32)
            days[c, :width, :] = shock.T
            days[c, width:, :] = (0.5 * (wide * wide)).astype(jnp.bfloat16).T

    def chunk_step(g, carry):
        @pl.when(g * CHUNK < live[0])
        def _():
            for copy in block_copies(g):
                copy.wait()
            for i in range(CHUNK):
                slot = g * CHUNK + i
                tile = lax.rem(desks[slot] - position + (REACH + devices), devices)
                block = jnp.concatenate([delta[slot], gamma[slot]], axis=1)
                block = jnp.where(slot < live[0], block, jnp.zeros_like(block))
                tiles[tile] += jnp.dot(block, days[columns[slot]], preferred_element_type=jnp.float32)

        return carry

    lax.fori_loop(0, slots // CHUNK, chunk_step, 0)
    copies = [pltpu.make_async_copy(tiles.at[t], out_hbm.at[t], out_sem.at[t]) for t in range(SPAN)]
    for copy in copies:
        copy.start()
    for copy in copies:
        copy.wait()


def split(value):
    high = value.astype(jnp.bfloat16)
    return high, (value - high.astype(jnp.float32)).astype(jnp.bfloat16)


def exchange_kernel(n, scale, ids_ref, tiles, pnl_ref, book_ref, even, paired, middle, landed, rows, pick,
                    load_sem, send1, recv1, send2, recv2, send3, recv3, send4, recv4):
    me = lax.axis_index("factor")
    core = lax.rem(me, 2)
    side = lax.rem(me // 2, 2)
    sibling = me + 1 - 2 * core
    partner = me + 2 - 4 * side
    half = even.shape[1] // PIECES
    parts = [pl.ds(h * half, half) for h in range(PIECES)]

    def at(distance):
        return {"factor": lax.rem(me + distance + n, n)}

    def remote(src, dst, send, recv, device):
        return pltpu.make_async_remote_copy(
            src_ref=src, dst_ref=dst, send_sem=send, recv_sem=recv,
            device_id=device, device_id_type=pl.DeviceIdType.MESH,
        )

    def place(k):
        return k + side * (4 - 2 * k)

    loads = [pltpu.make_async_copy(tiles.at[2 * e], even.at[e], load_sem.at[e]) for e in range(5)]
    for load in loads:
        load.start()

    barrier = pltpu.get_barrier_semaphore()
    for device in ({"factor": sibling}, {"factor": partner}, at(4), at(-4)):
        pl.semaphore_signal(barrier, inc=1, device_id=device, device_id_type=pl.DeviceIdType.MESH)
    pl.semaphore_wait(barrier, 4)

    def pair(i):
        return remote(tiles.at[2 * i + 1], paired.at[i], send1.at[i], recv1.at[i], {"factor": sibling})

    def if_paired(k, owner, act):
        if k == 0:
            pl.when(owner == 1 - side)(act)
        elif k == 4:
            pl.when(owner == side)(act)
        else:
            act()

    order = (0, 1, 3, 4, 2)
    for k in order:
        if_paired(k, 1 - core, lambda: pair(place(k) - core).start())
    for load in loads:
        load.wait()

    def add_pair(k):
        e = place(k)

        def act():
            i = e - 1 + core
            pair(i).wait_recv()
            even[e] += paired[i]

        if_paired(k, core, act)

    def straight(k, slot, part):
        e = place(k)
        return remote(even.at[e, part], landed.at[slot, part], send2.at[slot, part.start // half],
                      recv2.at[slot, part.start // half], at(2 * e - 4))

    def across(k, slot, part):
        return remote(even.at[place(k), part], middle.at[slot, part], send3.at[slot, part.start // half],
                      recv3.at[slot, part.start // half], {"factor": partner})

    add_pair(0)
    first = [straight(0, 0, part) for part in parts]
    for copy in first:
        copy.start()
    add_pair(1)
    joined = [across(1, 0, part) for part in parts]
    for copy in joined:
        copy.start()
    add_pair(3)
    owned = [across(3, 1, part) for part in parts]
    for copy in owned:
        copy.start()
    add_pair(4)
    add_pair(2)

    whole = (even[0] + even[1]) + (even[2] + even[3]) + even[4]
    rows[0] = jnp.sum(whole, axis=0, keepdims=True)
    near = [
        remote(rows.at[0], rows.at[1], send4.at[0], recv4.at[0], {"factor": sibling}),
        remote(rows.at[2], rows.at[3], send4.at[1], recv4.at[1], {"factor": partner}),
    ]
    near[0].start()

    second = [straight(4, 1, part) for part in parts]
    for h, part in enumerate(parts):
        joined[h].wait_recv()
        even[place(4), part] += middle[0, part]
        second[h].start()
    day = lax.broadcasted_iota(jnp.int32, pick.shape, 0)
    pick[...] = (day == ids_ref[...]).astype(jnp.float32).astype(jnp.bfloat16)
    near[0].wait()
    rows[2] = rows[0] + rows[1]
    near[1].start()
    near[1].wait()
    rows[4] = rows[2] + rows[3]
    total = rows[4]
    for k in range(n // 4 - 1):
        hop = remote(rows.at[4 + k], rows.at[5 + k], send4.at[2 + k], recv4.at[2 + k], at(4))
        hop.start()
        hop.wait()
        total += rows[5 + k]
    high, rest = split(jnp.broadcast_to(total, (16, total.shape[1])))
    book = jnp.dot(high, pick[...], preferred_element_type=jnp.float32)
    book += jnp.dot(rest, pick[...], preferred_element_type=jnp.float32)
    book_ref[...] = book[0:1] * scale

    for copy in owned + first:
        copy.wait()
    even[2] += middle[1] + landed[0]
    for copy in second:
        copy.wait()
    high, rest = split(even[2] + landed[1])
    pnl_ref[...] = jnp.dot(high, pick[...], preferred_element_type=jnp.float32) + jnp.dot(
        rest, pick[...], preferred_element_type=jnp.float32
    )
    for copy in joined:
        copy.wait_send()
    for k in order:
        if_paired(k, 1 - core, lambda: pair(place(k) - core).wait_send())


def per_device(devices, history, scenario_ids, desk_ids, column_ids, live_count, delta_blocks, gamma_blocks):
    day_count, factors = history.shape
    slots, desk_rows, width = delta_blocks.shape
    columns = factors // width
    scenarios = scenario_ids.shape[0]

    tiles = pl.pallas_call(
        functools.partial(block_kernel, devices),
        in_specs=[pl.BlockSpec(memory_space=pltpu.SMEM)] * 3 + [pl.BlockSpec(memory_space=pl.ANY)] * 3,
        out_specs=pl.BlockSpec(memory_space=pl.ANY),
        scratch_shapes=[
            pltpu.VMEM((SPAN, desk_rows, day_count), jnp.float32),
            pltpu.VMEM((columns, 2 * width, day_count), jnp.bfloat16),
            pltpu.VMEM((day_count, factors), jnp.bfloat16),
            pltpu.VMEM((slots, desk_rows, width), jnp.bfloat16),
            pltpu.VMEM((slots, desk_rows, width), jnp.bfloat16),
            pltpu.SemaphoreType.DMA((HIST_PARTS,)),
            pltpu.SemaphoreType.DMA((2, slots // CHUNK)),
            pltpu.SemaphoreType.DMA((SPAN,)),
        ],
        out_shape=jax.ShapeDtypeStruct((SPAN, desk_rows, day_count), jnp.float32),
        compiler_params=pltpu.CompilerParams(vmem_limit_bytes=62 * MIB),
        name="block_products",
    )(desk_ids, column_ids, live_count, history, delta_blocks, gamma_blocks)

    f32 = jnp.float32
    tile = (desk_rows, day_count)
    pnl, book = pl.pallas_call(
        functools.partial(exchange_kernel, devices, 1.0 / math.sqrt(devices * desk_rows)),
        in_specs=[pl.BlockSpec(memory_space=pltpu.VMEM), pl.BlockSpec(memory_space=pl.ANY)],
        out_specs=[pl.BlockSpec(memory_space=pltpu.VMEM)] * 2,
        out_shape=[
            jax.ShapeDtypeStruct((desk_rows, scenarios), f32),
            jax.ShapeDtypeStruct((1, scenarios), f32),
        ],
        scratch_shapes=[
            pltpu.VMEM((5, *tile), f32),
            pltpu.VMEM((4, *tile), f32),
            pltpu.VMEM((2, *tile), f32),
            pltpu.VMEM((2, *tile), f32),
            pltpu.VMEM((devices // 4 + 4, 1, day_count), f32),
            pltpu.VMEM((day_count, scenarios), jnp.bfloat16),
            pltpu.SemaphoreType.DMA((5,)),
            pltpu.SemaphoreType.DMA((4,)),
            pltpu.SemaphoreType.DMA((4,)),
            pltpu.SemaphoreType.DMA((2, PIECES)),
            pltpu.SemaphoreType.DMA((2, PIECES)),
            pltpu.SemaphoreType.DMA((2, PIECES)),
            pltpu.SemaphoreType.DMA((2, PIECES)),
            pltpu.SemaphoreType.DMA((devices // 4 + 1,)),
            pltpu.SemaphoreType.DMA((devices // 4 + 1,)),
        ],
        compiler_params=pltpu.CompilerParams(
            collective_id=0, has_side_effects=True, vmem_limit_bytes=40 * MIB
        ),
        name="desk_exchange",
    )(scenario_ids.reshape(1, scenarios), tiles)
    return pnl, book.reshape(scenarios)


def solution(mesh):
    return jax.shard_map(
        functools.partial(per_device, mesh.shape["factor"]),
        mesh=mesh,
        in_specs=(
            P(None, "factor"),
            P("groups"),
            P(("groups", "factor")),
            P(("groups", "factor")),
            P(("groups", "factor")),
            P(("groups", "factor"), None, None),
            P(("groups", "factor"), None, None),
        ),
        out_specs=(P(("groups", "factor"), None), P("groups")),
        check_vma=False,
    )
```

```python
import functools
import math

import jax
import jax.numpy as jnp
from jax import lax
from jax.experimental import pallas as pl
from jax.experimental.pallas import tpu as pltpu
from jax.sharding import PartitionSpec as P

REACH = 4
SPAN = 2 * REACH + 1
CHUNK = 16
HIST_PARTS = 4
PIECES = 2
MIB = 1 << 20


def block_kernel(devices, desks, columns, live, hist_hbm, delta_hbm, gamma_hbm, out_hbm,
                 tiles, days, hist, delta, gamma, hist_sem, block_sem, out_sem):
    position = lax.axis_index("factor")
    slots, _, width = delta.shape
    span = hist.shape[1] // hist_sem.shape[0]

    def hist_copy(h):
        at = pl.ds(h * span, span)
        return pltpu.make_async_copy(hist_hbm.at[:, at], hist.at[:, at], hist_sem.at[h])

    def block_copies(g):
        at = pl.ds(g * CHUNK, CHUNK)
        return [
            pltpu.make_async_copy(delta_hbm.at[at], delta.at[at], block_sem.at[0, g]),
            pltpu.make_async_copy(gamma_hbm.at[at], gamma.at[at], block_sem.at[1, g]),
        ]

    for h in range(hist_sem.shape[0]):
        hist_copy(h).start()
    for g in range(slots // CHUNK):

        @pl.when(g * CHUNK < live[0])
        def _():
            for copy in block_copies(g):
                copy.start()

    tiles[...] = jnp.zeros_like(tiles)
    for h in range(hist_sem.shape[0]):
        hist_copy(h).wait()
        for c in range(h * span // width, (h + 1) * span // width):
            shock = hist[:, c * width:(c + 1) * width]
            wide = shock.astype(jnp.float32)
            days[c, :width, :] = shock.T
            days[c, width:, :] = (0.5 * (wide * wide)).astype(jnp.bfloat16).T

    def chunk_step(g, carry):
        @pl.when(g * CHUNK < live[0])
        def _():
            for copy in block_copies(g):
                copy.wait()
            for i in range(CHUNK):
                slot = g * CHUNK + i
                tile = lax.rem(desks[slot] - position + (REACH + devices), devices)
                block = jnp.concatenate([delta[slot], gamma[slot]], axis=1)
                block = jnp.where(slot < live[0], block, jnp.zeros_like(block))
                tiles[tile] += jnp.dot(block, days[columns[slot]], preferred_element_type=jnp.float32)

        return carry

    lax.fori_loop(0, slots // CHUNK, chunk_step, 0)
    copies = [pltpu.make_async_copy(tiles.at[t], out_hbm.at[t], out_sem.at[t]) for t in range(SPAN)]
    for copy in copies:
        copy.start()
    for copy in copies:
        copy.wait()


def split(value):
    high = value.astype(jnp.bfloat16)
    return high, (value - high.astype(jnp.float32)).astype(jnp.bfloat16)


def exchange_kernel(n, scale, ids_ref, tiles, pnl_ref, book_ref, even, paired, middle, landed, rows, pick,
                    load_sem, send1, recv1, send2, recv2, send3, recv3, send4, recv4):
    me = lax.axis_index("factor")
    core = lax.rem(me, 2)
    side = lax.rem(me // 2, 2)
    sibling = me + 1 - 2 * core
    partner = me + 2 - 4 * side
    half = even.shape[1] // PIECES
    parts = [pl.ds(h * half, half) for h in range(PIECES)]

    def at(distance):
        return {"factor": lax.rem(me + distance + n, n)}

    def remote(src, dst, send, recv, device):
        return pltpu.make_async_remote_copy(
            src_ref=src, dst_ref=dst, send_sem=send, recv_sem=recv,
            device_id=device, device_id_type=pl.DeviceIdType.MESH,
        )

    def place(k):
        return k + side * (4 - 2 * k)

    loads = [pltpu.make_async_copy(tiles.at[2 * e], even.at[e], load_sem.at[e]) for e in range(5)]
    for load in loads:
        load.start()

    barrier = pltpu.get_barrier_semaphore()
    for k in range(1, n):
        pl.semaphore_signal(barrier, inc=1, device_id=at(k), device_id_type=pl.DeviceIdType.MESH)
    pl.semaphore_wait(barrier, n - 1)

    def pair(i):
        return remote(tiles.at[2 * i + 1], paired.at[i], send1.at[i], recv1.at[i], {"factor": sibling})

    def if_paired(k, owner, act):
        if k == 0:
            pl.when(owner == 1 - side)(act)
        elif k == 4:
            pl.when(owner == side)(act)
        else:
            act()

    order = (0, 1, 3, 4, 2)
    for k in order:
        if_paired(k, 1 - core, lambda: pair(place(k) - core).start())
    for load in loads:
        load.wait()

    def add_pair(k):
        e = place(k)

        def act():
            i = e - 1 + core
            pair(i).wait_recv()
            even[e] += paired[i]

        if_paired(k, core, act)

    def straight(k, slot, part):
        e = place(k)
        return remote(even.at[e, part], landed.at[slot, part], send2.at[slot, part.start // half],
                      recv2.at[slot, part.start // half], at(2 * e - 4))

    def across(k, slot, part):
        return remote(even.at[place(k), part], middle.at[slot, part], send3.at[slot, part.start // half],
                      recv3.at[slot, part.start // half], {"factor": partner})

    add_pair(0)
    first = [straight(0, 0, part) for part in parts]
    for copy in first:
        copy.start()
    add_pair(1)
    joined = [across(1, 0, part) for part in parts]
    for copy in joined:
        copy.start()
    add_pair(3)
    owned = [across(3, 1, part) for part in parts]
    for copy in owned:
        copy.start()
    add_pair(4)
    add_pair(2)

    whole = (even[0] + even[1]) + (even[2] + even[3]) + even[4]
    rows[0] = jnp.sum(whole, axis=0, keepdims=True)
    share = [remote(rows.at[0], rows.at[k], send4.at[k], recv4.at[k], at(k)) for k in range(1, n)]
    for copy in share:
        copy.start()

    second = [straight(4, 1, part) for part in parts]
    for h, part in enumerate(parts):
        joined[h].wait_recv()
        even[place(4), part] += middle[0, part]
        second[h].start()
    day = lax.broadcasted_iota(jnp.int32, pick.shape, 0)
    pick[...] = (day == ids_ref[...]).astype(jnp.float32).astype(jnp.bfloat16)
    for copy in share:
        copy.wait()
    total = rows[0]
    for k in range(1, n):
        total += rows[k]
    high, rest = split(jnp.broadcast_to(total, (16, total.shape[1])))
    book = jnp.dot(high, pick[...], preferred_element_type=jnp.float32)
    book += jnp.dot(rest, pick[...], preferred_element_type=jnp.float32)
    book_ref[...] = book[0:1] * scale

    for copy in owned + first:
        copy.wait()
    even[2] += middle[1] + landed[0]
    for copy in second:
        copy.wait()
    high, rest = split(even[2] + landed[1])
    pnl_ref[...] = jnp.dot(high, pick[...], preferred_element_type=jnp.float32) + jnp.dot(
        rest, pick[...], preferred_element_type=jnp.float32
    )
    for copy in joined:
        copy.wait_send()
    for k in order:
        if_paired(k, 1 - core, lambda: pair(place(k) - core).wait_send())


def per_device(devices, history, scenario_ids, desk_ids, column_ids, live_count, delta_blocks, gamma_blocks):
    day_count, factors = history.shape
    slots, desk_rows, width = delta_blocks.shape
    columns = factors // width
    scenarios = scenario_ids.shape[0]

    tiles = pl.pallas_call(
        functools.partial(block_kernel, devices),
        in_specs=[pl.BlockSpec(memory_space=pltpu.SMEM)] * 3 + [pl.BlockSpec(memory_space=pl.ANY)] * 3,
        out_specs=pl.BlockSpec(memory_space=pl.ANY),
        scratch_shapes=[
            pltpu.VMEM((SPAN, desk_rows, day_count), jnp.float32),
            pltpu.VMEM((columns, 2 * width, day_count), jnp.bfloat16),
            pltpu.VMEM((day_count, factors), jnp.bfloat16),
            pltpu.VMEM((slots, desk_rows, width), jnp.bfloat16),
            pltpu.VMEM((slots, desk_rows, width), jnp.bfloat16),
            pltpu.SemaphoreType.DMA((HIST_PARTS,)),
            pltpu.SemaphoreType.DMA((2, slots // CHUNK)),
            pltpu.SemaphoreType.DMA((SPAN,)),
        ],
        out_shape=jax.ShapeDtypeStruct((SPAN, desk_rows, day_count), jnp.float32),
        compiler_params=pltpu.CompilerParams(vmem_limit_bytes=63 * MIB),
        name="block_products",
    )(desk_ids, column_ids, live_count, history, delta_blocks, gamma_blocks)

    f32 = jnp.float32
    tile = (desk_rows, day_count)
    pnl, book = pl.pallas_call(
        functools.partial(exchange_kernel, devices, 1.0 / math.sqrt(devices * desk_rows)),
        in_specs=[pl.BlockSpec(memory_space=pltpu.VMEM), pl.BlockSpec(memory_space=pl.ANY)],
        out_specs=[pl.BlockSpec(memory_space=pltpu.VMEM)] * 2,
        out_shape=[
            jax.ShapeDtypeStruct((desk_rows, scenarios), f32),
            jax.ShapeDtypeStruct((1, scenarios), f32),
        ],
        scratch_shapes=[
            pltpu.VMEM((5, *tile), f32),
            pltpu.VMEM((4, *tile), f32),
            pltpu.VMEM((2, *tile), f32),
            pltpu.VMEM((2, *tile), f32),
            pltpu.VMEM((devices, 1, day_count), f32),
            pltpu.VMEM((day_count, scenarios), jnp.bfloat16),
            pltpu.SemaphoreType.DMA((5,)),
            pltpu.SemaphoreType.DMA((4,)),
            pltpu.SemaphoreType.DMA((4,)),
            pltpu.SemaphoreType.DMA((2, PIECES)),
            pltpu.SemaphoreType.DMA((2, PIECES)),
            pltpu.SemaphoreType.DMA((2, PIECES)),
            pltpu.SemaphoreType.DMA((2, PIECES)),
            pltpu.SemaphoreType.DMA((devices,)),
            pltpu.SemaphoreType.DMA((devices,)),
        ],
        compiler_params=pltpu.CompilerParams(
            collective_id=0, has_side_effects=True, vmem_limit_bytes=62 * MIB
        ),
        name="desk_exchange",
    )(scenario_ids.reshape(1, scenarios), tiles)
    return pnl, book.reshape(scenarios)


def solution(mesh):
    return jax.shard_map(
        functools.partial(per_device, mesh.shape["factor"]),
        mesh=mesh,
        in_specs=(
            P(None, "factor"),
            P("groups"),
            P(("groups", "factor")),
            P(("groups", "factor")),
            P(("groups", "factor")),
            P(("groups", "factor"), None, None),
            P(("groups", "factor"), None, None),
        ),
        out_specs=(P(("groups", "factor"), None), P("groups")),
        check_vma=False,
    )
```
